512 devices in a mesh: space: 32 (over x_hi, z), modes: 16 (over y, x_lo, core).
Axes of the slice: x: 4 (x_hi: 2, x_lo: 2; x = x_hi * 2 + x_lo), y: 4, z: 16, core: 2. Of those that a mesh axis runs over, the one named last changes fastest.
Arguments:
- mode_field: bfloat16 [64, 128, 256, 256], P('space', 'modes'), may hold values from -8 to 8
- diffusion: float32 [64, 256, 256], P('space'), may hold values from 0.1 to 0.16
- joule_load: float32 [64, 256, 256], P('space'), may hold values from 0.5 to 1.5
- chaos_basis: bfloat16 [343, 128], replicated, may hold values from -0.5 to 0.5
- quad_weight: float32 [343], replicated, may hold values from 0.25 to 1
- base_conductivity: float32 [343], replicated, may hold values from 0.5 to 2
- thermal_slope: float32 [343], replicated, may hold values from 0.2 to 0.8
Outputs:
- advanced: bfloat16 [64, 128, 256, 256], P('space', 'modes')
The draws below stay inside these ranges and needn't reach their ends.
All inputs are finite; a program needn't handle non-finite values.
Results may differ from the reference program's by a relative error of at most 0.0054.
Values may be sent and summed in bfloat16 or wider, within the bound.
A program may use at most 64 MiB of HBM per device.

```python
import math
import jax
import jax.numpy as jnp
from jax import lax

MODES = 128
Q = 343
NX = 256
NY = 256
NZ = 64


def draw_mode_field(key, part):
    noise_key = jax.random.fold_in(key, 11)
    amplitude_key = jax.random.fold_in(key, 12)
    count_key = jax.random.fold_in(key, 13)
    phase_key = jax.random.fold_in(key, 14)
    full_shape = (NZ, MODES, NX, NY)
    rough_part = jnp.clip(jax.random.normal(noise_key, full_shape, jnp.float32), -2.5, 2.5)
    amplitude = jax.random.uniform(amplitude_key, (MODES,), jnp.float32, 0.6, 2.0)
    wave_count = jax.random.randint(count_key, (3, MODES), 1, 3).astype(jnp.float32)
    phase_shift = jax.random.uniform(phase_key, (3, MODES), jnp.float32, 0.0, 2.0 * math.pi)
    depth_coord = (jnp.arange(NZ, dtype=jnp.float32) + 0.5) / NZ
    row_coord = (jnp.arange(NX, dtype=jnp.float32) + 0.5) / NX
    column_coord = (jnp.arange(NY, dtype=jnp.float32) + 0.5) / NY
    depth_wave = jnp.sin(2.0 * math.pi * depth_coord[:, None] * wave_count[0][None, :] + phase_shift[0][None, :])
    row_wave = jnp.sin(2.0 * math.pi * wave_count[1][:, None] * row_coord[None, :] + phase_shift[1][:, None])
    column_wave = jnp.sin(2.0 * math.pi * wave_count[2][:, None] * column_coord[None, :] + phase_shift[2][:, None])
    summed_waves = depth_wave[:, :, None, None] + row_wave[None, :, :, None] + column_wave[None, :, None, :]
    smooth_part = amplitude[None, :, None, None] * summed_waves / 1.2247
    return (smooth_part + rough_part).astype(jnp.bfloat16)


def level_of(key, extent, pieces, least, top_value):
    def one(dim, parts):
        draws = jax.random.uniform(jax.random.fold_in(jax.random.fold_in(key, 6), dim), (parts,), jnp.float32, least / len(pieces), top_value / len(pieces))
        return jnp.repeat(jnp.exp(draws), extent[dim] // parts).reshape((-1,) + (1,) * (len(extent) - dim - 1))

    level = one(*pieces[0])
    for cut in pieces[1:]:
        level = level * one(*cut)
    return level


def bell_draw(rng, dims, width, bound, held_as=jnp.bfloat16):
    entries = jax.random.normal(rng, dims, jnp.float32) * width
    return jnp.minimum(jnp.maximum(entries, -bound), bound).astype(held_as)


def setup_inputs(seed: int = 0) -> dict:
    seeds = jax.random.split(jax.random.key(seed), 8)
    return {
        "mode_field": draw_mode_field(jax.random.fold_in(seeds[7], 71), 0),
        "diffusion": jnp.clip(0.1 + 0.059999995 * jax.random.uniform(seeds[1], (NZ, NX, NY), jnp.float32) ** level_of(seeds[1], (NZ, NX, NY), ((0, 32),), -0.2, 0.2), 0.1, 0.16),
        "joule_load": jnp.clip(0.5 + 1.0 * jax.random.uniform(seeds[2], (NZ, NX, NY), jnp.float32) ** level_of(seeds[2], (NZ, NX, NY), ((0, 32),), -0.2, 0.2), 0.5, 1.5),
        "chaos_basis": bell_draw(seeds[3], (Q, MODES), MODES ** -0.5, 0.5),
        "quad_weight": jnp.clip(jnp.exp(jax.random.uniform(seeds[4], (Q,), jnp.float32, math.log(0.25), math.log(1.0))), 0.25, 1.0),
        "base_conductivity": jnp.clip(jnp.exp(jax.random.uniform(seeds[5], (Q,), jnp.float32, math.log(0.5), math.log(2.0))), 0.5, 2.0),
        "thermal_slope": jnp.clip(jax.random.uniform(seeds[6], (Q,), jnp.float32, 0.2, 0.8), 0.2, 0.8),
    }


def transport(values, diffusion):
    for sweep in range(2):
        padded = jnp.pad(values, 1)
        beside = padded[2:, 1:-1, 1:-1] + padded[:-2, 1:-1, 1:-1]
        beside = beside + padded[1:-1, 2:, 1:-1] + padded[1:-1, :-2, 1:-1]
        beside = beside + padded[1:-1, 1:-1, 2:] + padded[1:-1, 1:-1, :-2]
        values = values + diffusion * (beside - 6.0 * values)
    return values.astype(jnp.bfloat16)


def reference(mode_field, diffusion, joule_load, chaos_basis, quad_weight, base_conductivity, thermal_slope):
    moved = lax.map(lambda single: transport(single.astype(jnp.float32), diffusion), jnp.swapaxes(mode_field, 0, 1))
    moved = jnp.swapaxes(moved, 0, 1)
    basis_wide = chaos_basis.astype(jnp.float32)

    def per_plane(pair):
        plane, load_plane = pair
        point_temp = jnp.einsum("qm,mxy->qxy", basis_wide, plane.astype(jnp.float32), precision=lax.Precision.HIGHEST)
        conductivity = base_conductivity[:, None, None] * (1.0 + thermal_slope[:, None, None] * jnp.tanh(point_temp))
        weighted = (quad_weight[:, None, None] * conductivity).astype(jnp.bfloat16)
        projected = jnp.einsum("qm,qxy->mxy", basis_wide, weighted.astype(jnp.float32), precision=lax.Precision.HIGHEST).astype(jnp.bfloat16)
        kept_modes = lax.optimization_barrier(plane).astype(jnp.float32)
        return (kept_modes + load_plane[None] * projected.astype(jnp.float32)).astype(jnp.bfloat16)

    return lax.map(per_plane, (moved, joule_load))
```

```python
import functools

import jax
import jax.numpy as jnp
from jax import lax
from jax.experimental import pallas as pl
from jax.experimental.pallas import tpu as pltpu
from jax.sharding import PartitionSpec as P

MESH = pl.DeviceIdType.MESH
F32 = jnp.float32
BF16 = jnp.bfloat16

NX = 256
NY = 256
LANES = 128
GROUPS = NX // 16
DEV = 16
SPACE = 32
CHUNKS = 4
E = NX // CHUNKS
R = E // DEV
QP = 352


def halves(row):
    return row[..., :LANES], row[..., LANES:]


def beside_y(low, high, first_lane, last_lane):
    up_l, up_h = pltpu.roll(low, 1, 1), pltpu.roll(high, 1, 1)
    dn_l, dn_h = pltpu.roll(low, LANES - 1, 1), pltpu.roll(high, LANES - 1, 1)
    sum_l = jnp.where(first_lane, 0.0, up_l) + jnp.where(last_lane, dn_h, dn_l)
    sum_h = jnp.where(first_lane, up_l, up_h) + jnp.where(last_lane, 0.0, dn_h)
    return sum_l, sum_h


def swap_planes(a):
    return jnp.concatenate([a[8:], a[:8]], axis=0)


def spread(tile0, tile1, k):
    return jnp.concatenate(
        [
            jnp.broadcast_to(tile0[k : k + 1], (8, LANES)),
            jnp.broadcast_to(tile1[k : k + 1], (8, LANES)),
        ],
        axis=0,
    )


def kernel(
    v_ref, d_ref, joule_ref, w1_ref, w2_ref, bias_ref, out_ref,
    to_l, to_r, from_l, from_r, part, first, settled, gathered, projected, returned,
    halo_send, halo_recv, fwd_send, fwd_recv, back_send, back_recv,
):
    s = lax.axis_index("space")
    m = lax.axis_index("modes")

    barrier = pltpu.get_barrier_semaphore()

    def greet(k, _):
        pl.semaphore_signal(
            barrier, inc=1, device_id=(s, lax.rem(m + k, DEV)), device_id_type=MESH
        )
        return 0

    lax.fori_loop(1, DEV, greet, 0)

    @pl.when(s > 0)
    def _():
        pl.semaphore_signal(barrier, inc=1, device_id=(s - 1, m), device_id_type=MESH)

    @pl.when(s < SPACE - 1)
    def _():
        pl.semaphore_signal(barrier, inc=1, device_id=(s + 1, m), device_id_type=MESH)

    lane = lax.broadcasted_iota(jnp.int32, (16, LANES), 1)
    first_lane, last_lane = lane == 0, lane == LANES - 1

    def row_of(ref, x):
        return halves(ref[x].astype(F32))

    def sweep_group(g, _):
        x0 = g * 16
        before = row_of(v_ref, lax.rem(x0 + NX - 1, NX))
        before = tuple(jnp.where(g == 0, 0.0, b) for b in before)
        after = row_of(v_ref, lax.rem(x0 + 16, NX))
        after = tuple(jnp.where(g == GROUPS - 1, 0.0, a) for a in after)
        rows = [before] + [row_of(v_ref, x0 + k) for k in range(16)] + [after]
        rate = [halves(d_ref[z, pl.ds(x0, 16), :]) for z in range(2)]
        for k in range(16):
            here = rows[k + 1]
            across = beside_y(*here, first_lane, last_lane)
            for h in range(2):
                mid = here[h]
                sides = rows[k][h] + rows[k + 2][h] + across[h] + swap_planes(mid)
                g_row = mid + spread(rate[0][h], rate[1][h], k) * (sides - 6.0 * mid)
                cols = pl.ds(h * LANES, LANES)
                part[x0 + k, :, cols] = g_row
                to_l[g, k, :, cols] = jnp.concatenate([mid[:8], g_row[:8]], axis=0).astype(BF16)
                to_r[g, k, :, cols] = jnp.concatenate([mid[8:], g_row[8:]], axis=0).astype(BF16)
        to_l[g, 16] = d_ref[0, pl.ds(x0, 16), :].astype(BF16)
        to_r[g, 16] = d_ref[1, pl.ds(x0, 16), :].astype(BF16)
        return 0

    def span(c):
        a = 0 if c == 0 else c * (E // 16) + 1
        b = GROUPS if c == CHUNKS - 1 else (c + 1) * (E // 16) + 1
        return a, b - a

    def halo_copies(c):
        a, n = span(c)
        left = pltpu.make_async_remote_copy(
            src_ref=to_l.at[pl.ds(a, n)],
            dst_ref=from_r.at[pl.ds(a, n)],
            send_sem=halo_send.at[0, c],
            recv_sem=halo_recv.at[0, c],
            device_id=(s - 1, m),
            device_id_type=MESH,
        )
        right = pltpu.make_async_remote_copy(
            src_ref=to_r.at[pl.ds(a, n)],
            dst_ref=from_l.at[pl.ds(a, n)],
            send_sem=halo_send.at[1, c],
            recv_sem=halo_recv.at[1, c],
            device_id=(s + 1, m),
            device_id_type=MESH,
        )
        return left, right

    @pl.when(s == 0)
    def _():
        def clear(g, _):
            from_l[g] = jnp.zeros((17, 16, NY), BF16)
            return 0

        lax.fori_loop(0, GROUPS, clear, 0)

    @pl.when(s == SPACE - 1)
    def _():
        def clear(g, _):
            from_r[g] = jnp.zeros((17, 16, NY), BF16)
            return 0

        lax.fori_loop(0, GROUPS, clear, 0)

    first[0] = jnp.zeros((16, NY), F32)
    first[NX + 1] = jnp.zeros((16, NY), F32)

    for c in range(CHUNKS):
        a, n = span(c)
        lax.fori_loop(a, a + n, sweep_group, 0)
        if c == 0:
            inner = (s > 0) & (s < SPACE - 1)

            @pl.when(inner)
            def _():
                pl.semaphore_wait(barrier, DEV + 1)

            @pl.when(jnp.logical_not(inner))
            def _():
                pl.semaphore_wait(barrier, DEV)

        left, right = halo_copies(c)
        pl.when(s > 0)(left.start)
        pl.when(s < SPACE - 1)(right.start)

    def finish_group(g, _):
        x0 = g * 16
        rate = [halves(d_ref[z, pl.ds(x0, 16), :]) for z in range(2)]
        for k in range(16):
            near_l, near_r = from_l[g, k], from_r[g, k]
            for h in range(2):
                cols = pl.ds(h * LANES, LANES)
                vl = near_l[:, h * LANES : (h + 1) * LANES].astype(F32)
                vr = near_r[:, h * LANES : (h + 1) * LANES].astype(F32)
                outer = jnp.concatenate([vl[:8], vr[:8]], axis=0)
                first[x0 + k + 1, :, cols] = (
                    part[x0 + k, :, cols] + spread(rate[0][h], rate[1][h], k) * outer
                )
        return 0

    def second_group(g, _):
        x0 = g * 16
        rate = [halves(d_ref[z, pl.ds(x0, 16), :]) for z in range(2)]
        outer_rate = [halves(ref[g, 16].astype(F32)) for ref in (from_l, from_r)]
        rows = [halves(first[x0 + k]) for k in range(18)]
        for k in range(16):
            here = rows[k + 1]
            across = beside_y(*here, first_lane, last_lane)
            v_row = row_of(v_ref, x0 + k)
            near_l, near_r = row_of(from_l.at[g], k), row_of(from_r.at[g], k)
            for h in range(2):
                mid = here[h]
                outer = jnp.concatenate([near_l[h][8:], near_r[h][8:]], axis=0)
                outer = outer + spread(outer_rate[0][h], outer_rate[1][h], k) * v_row[h]
                sides = rows[k][h] + rows[k + 2][h] + across[h] + swap_planes(mid) + outer
                value = mid + spread(rate[0][h], rate[1][h], k) * (sides - 6.0 * mid)
                settled[x0 + k, :, pl.ds(h * LANES, LANES)] = value.astype(BF16)
        return 0

    def fwd_copy(c, j, send=fwd_send, recv=fwd_recv):
        return pltpu.make_async_remote_copy(
            src_ref=settled.at[pl.ds(c * E + j * R, R)],
            dst_ref=gathered.at[c, m],
            send_sem=send.at[c],
            recv_sem=recv.at[c],
            device_id=(s, j),
            device_id_type=MESH,
        )

    def back_copy(c, j):
        return pltpu.make_async_remote_copy(
            src_ref=projected.at[c, j],
            dst_ref=returned.at[pl.ds(c * E + m * R, R)],
            send_sem=back_send.at[c],
            recv_sem=back_recv.at[c],
            device_id=(s, j),
            device_id_type=MESH,
        )

    def stage_stencil(c):
        for chunk in range(CHUNKS):

            @pl.when(c == chunk)
            def _():
                left, right = halo_copies(chunk)
                pl.when(s < SPACE - 1)(left.wait_recv)
                pl.when(s > 0)(right.wait_recv)
                a, n = span(chunk)
                lax.fori_loop(a, a + n, finish_group, 0)

        n = E // 16
        lax.fori_loop(c * n, (c + 1) * n, second_group, 0)

        def send(k, _):
            fwd_copy(c, lax.rem(m + k, DEV)).start()
            return 0

        lax.fori_loop(1, DEV, send, 0)
        pltpu.make_async_copy(
            settled.at[pl.ds(c * E + m * R, R)], gathered.at[c, m], fwd_recv.at[c]
        ).start()

    def stage_evaluate(c):
        pltpu.make_async_copy(gathered.at[c], gathered.at[c], fwd_recv.at[c]).wait()

        def one(r, _):
            cells = gathered[c, :, r].reshape(16 * DEV, NY)
            temp = jnp.dot(w1_ref[...], cells, preferred_element_type=F32)
            heat = jnp.tanh(temp).astype(BF16)
            source = jnp.dot(w2_ref[...], heat, preferred_element_type=F32)
            source = source + bias_ref[:, :1]
            projected[c, :, r] = source.astype(BF16).reshape(DEV, 16, NY)
            return 0

        lax.fori_loop(0, R, one, 0)

        def send(k, _):
            back_copy(c, lax.rem(m + k, DEV)).start()
            return 0

        lax.fori_loop(1, DEV, send, 0)
        pltpu.make_async_copy(
            projected.at[c, m], returned.at[pl.ds(c * E + m * R, R)], back_recv.at[c]
        ).start()

    def stage_finish(c):
        rows = returned.at[pl.ds(c * E, E)]
        pltpu.make_async_copy(rows, rows, back_recv.at[c]).wait()

        def group(g, _):
            x0 = g * 16
            load = [halves(joule_ref[z, pl.ds(x0, 16), :]) for z in range(2)]
            for k in range(16):
                kept, source = row_of(settled, x0 + k), row_of(returned, x0 + k)
                for h in range(2):
                    value = kept[h] + spread(load[0][h], load[1][h], k) * source[h]
                    out_ref[x0 + k, :, pl.ds(h * LANES, LANES)] = value.astype(BF16)
            return 0

        n = E // 16
        lax.fori_loop(c * n, (c + 1) * n, group, 0)

    def step(t, _):
        @pl.when(t < CHUNKS)
        def _():
            stage_stencil(t)

        @pl.when((t >= 1) & (t < CHUNKS + 1))
        def _():
            stage_evaluate(t - 1)

        @pl.when(t >= 2)
        def _():
            stage_finish(t - 2)

        return 0

    lax.fori_loop(0, CHUNKS + 2, step, 0)

    for c in range(CHUNKS):
        left, right = halo_copies(c)
        pl.when(s > 0)(left.wait_send)
        pl.when(s < SPACE - 1)(right.wait_send)
        sent = settled.at[pl.ds(0, (DEV - 1) * R)]
        pltpu.make_async_copy(sent, sent, fwd_send.at[c]).wait()
        pltpu.make_async_copy(sent, sent, back_send.at[c]).wait()


def on_device(
    mode_field, diffusion, joule_load, chaos_basis, quad_weight, base_conductivity, thermal_slope
):
    planes, modes = mode_field.shape[:2]
    points = chaos_basis.shape[0]
    field = jnp.transpose(mode_field, (2, 0, 1, 3)).reshape(NX, planes * modes, NY)

    level = quad_weight * base_conductivity
    swing = level * thermal_slope
    basis = chaos_basis.astype(F32)
    eye = jnp.eye(planes, dtype=F32)
    pad = ((0, QP - points), (0, 0))
    split = jnp.pad(basis, pad).reshape(QP, DEV, modes)
    w1 = split[None, :, :, None, :] * eye[:, None, None, :, None]
    w1 = w1.reshape(planes * QP, DEV * planes * modes).astype(BF16)
    split = jnp.pad(basis * swing[:, None], pad).reshape(QP, DEV, modes)
    split = jnp.transpose(split, (1, 2, 0))
    w2 = split[:, None, :, None, :] * eye[None, :, None, :, None]
    w2 = w2.reshape(DEV * planes * modes, planes * QP).astype(BF16)
    bias = jnp.sum(basis * level[:, None], axis=0).reshape(DEV, 1, modes, 1)
    bias = jnp.broadcast_to(bias, (DEV, planes, modes, LANES)).reshape(-1, LANES)

    vmem = pl.BlockSpec(memory_space=pltpu.VMEM)
    rows16 = (NX, 16, NY)
    halo = (GROUPS, 17, 16, NY)
    out = pl.pallas_call(
        kernel,
        out_shape=jax.ShapeDtypeStruct(rows16, BF16),
        in_specs=[vmem] * 6,
        out_specs=vmem,
        scratch_shapes=[
            pltpu.VMEM(halo, BF16),
            pltpu.VMEM(halo, BF16),
            pltpu.VMEM(halo, BF16),
            pltpu.VMEM(halo, BF16),
            pltpu.VMEM(rows16, F32),
            pltpu.VMEM((NX + 2, 16, NY), F32),
            pltpu.VMEM(rows16, BF16),
            pltpu.VMEM((CHUNKS, DEV, R, 16, NY), BF16),
            pltpu.VMEM((CHUNKS, DEV, R, 16, NY), BF16),
            pltpu.VMEM(rows16, BF16),
            pltpu.SemaphoreType.DMA((2, CHUNKS)),
            pltpu.SemaphoreType.DMA((2, CHUNKS)),
            pltpu.SemaphoreType.DMA((CHUNKS,)),
            pltpu.SemaphoreType.DMA((CHUNKS,)),
            pltpu.SemaphoreType.DMA((CHUNKS,)),
            pltpu.SemaphoreType.DMA((CHUNKS,)),
        ],
        compiler_params=pltpu.CompilerParams(
            collective_id=0, has_side_effects=True, vmem_limit_bytes=56 * 2**20
        ),
        cost_estimate=pl.CostEstimate(
            flops=3 * 10**9, bytes_accessed=6 * 2**20, transcendentals=3 * 10**6
        ),
    )(field, diffusion, joule_load, w1, w2, bias)
    return jnp.transpose(out.reshape(NX, planes, modes, NY), (1, 2, 0, 3))


def solution(mesh):
    return jax.shard_map(
        on_device,
        mesh=mesh,
        in_specs=(
            P("space", "modes", None, None),
            P("space", None, None),
            P("space", None, None),
            P(),
            P(),
            P(),
            P(),
        ),
        out_specs=P("space", "modes", None, None),
        check_vma=False,
    )
```

```python
import functools

import jax
import jax.numpy as jnp
from jax import lax
from jax.experimental import pallas as pl
from jax.experimental.pallas import tpu as pltpu
from jax.sharding import PartitionSpec as P

MESH = pl.DeviceIdType.MESH
F32 = jnp.float32
BF16 = jnp.bfloat16

NX = 256
NY = 256
LANES = 128
GROUPS = NX // 16
DEV = 16
SPACE = 32
FAR = SPACE // 2
CHUNKS = 8
E = NX // CHUNKS
R = E // DEV
QP = 352


def halves(row):
    return row[..., :LANES], row[..., LANES:]


def beside_y(low, high, first_lane, last_lane):
    up_l, up_h = pltpu.roll(low, 1, 1), pltpu.roll(high, 1, 1)
    dn_l, dn_h = pltpu.roll(low, LANES - 1, 1), pltpu.roll(high, LANES - 1, 1)
    sum_l = jnp.where(first_lane, 0.0, up_l) + jnp.where(last_lane, dn_h, dn_l)
    sum_h = jnp.where(first_lane, up_l, up_h) + jnp.where(last_lane, 0.0, dn_h)
    return sum_l, sum_h


def swap_planes(a):
    return jnp.concatenate([a[8:], a[:8]], axis=0)


def spread(tile0, tile1, k):
    return jnp.concatenate(
        [
            jnp.broadcast_to(tile0[k : k + 1], (8, LANES)),
            jnp.broadcast_to(tile1[k : k + 1], (8, LANES)),
        ],
        axis=0,
    )


def kernel(
    field_ref, d_ref, joule_ref, basis_ref, weight_ref, base_ref, slope_ref, out_ref,
    v_ref, swap,
    to_l, to_r, from_l, from_r, relayed, part, first, settled, gathered, projected, returned,
    w1, w2, bias,
    halo_send, halo_recv, relay_recv, fwd_send, fwd_recv, back_send, back_recv,
):
    s = lax.axis_index("space")
    m = lax.axis_index("modes")

    barrier = pltpu.get_barrier_semaphore()

    def greet(k, _):
        pl.semaphore_signal(
            barrier, inc=1, device_id=(s, lax.rem(m + k, DEV)), device_id_type=MESH
        )
        return 0

    lax.fori_loop(1, DEV, greet, 0)

    @pl.when(s > 0)
    def _():
        pl.semaphore_signal(barrier, inc=1, device_id=(s - 1, m), device_id_type=MESH)

    @pl.when(s < SPACE - 1)
    def _():
        pl.semaphore_signal(barrier, inc=1, device_id=(s + 1, m), device_id_type=MESH)

    is_end = (s == 0) | (s == SPACE - 1)
    is_far = (s == FAR - 1) | (s == FAR)
    by_relay = (lax.rem(m, 2) == 1) & (is_end | is_far)
    across = lax.rem(s + FAR, SPACE)
    around = lax.rem(s // FAR * 2 * FAR + FAR + SPACE - 1 - s, SPACE)

    @pl.when(by_relay)
    def _():
        pl.semaphore_signal(barrier, inc=1, device_id=(across, m), device_id_type=MESH)
        pl.semaphore_signal(barrier, inc=1, device_id=(around, m), device_id_type=MESH)

    lane = lax.broadcasted_iota(jnp.int32, (16, LANES), 1)
    first_lane, last_lane = lane == 0, lane == LANES - 1

    def row_of(ref, x):
        return halves(ref[x].astype(F32))

    to_row = lax.broadcasted_iota(jnp.int32, (256, 256), 0)
    from_row = lax.broadcasted_iota(jnp.int32, (256, 256), 1)
    swapped = (to_row // 16 == from_row % 16) & (to_row % 16 == from_row // 16)
    swap[...] = jnp.where(swapped, 1.0, 0.0).astype(BF16)

    def regroup(g):
        x0 = g * 16
        block = field_ref[:, :, pl.ds(x0, 16), :].reshape(256, NY)
        rows = jnp.dot(swap[...], block, preferred_element_type=F32)
        v_ref[pl.ds(x0, 16)] = rows.astype(BF16).reshape(16, 16, NY)

    regroup(0)

    def sweep_group(g, _):
        x0 = g * 16
        regroup(lax.rem(g + 1, GROUPS))
        before = row_of(v_ref, lax.rem(x0 + NX - 1, NX))
        before = tuple(jnp.where(g == 0, 0.0, b) for b in before)
        after = row_of(v_ref, lax.rem(x0 + 16, NX))
        after = tuple(jnp.where(g == GROUPS - 1, 0.0, a) for a in after)
        rows = [before] + [row_of(v_ref, x0 + k) for k in range(16)] + [after]
        rate = [halves(d_ref[z, pl.ds(x0, 16), :]) for z in range(2)]
        for k in range(16):
            here = rows[k + 1]
            across = beside_y(*here, first_lane, last_lane)
            for h in range(2):
                mid = here[h]
                sides = rows[k][h] + rows[k + 2][h] + across[h] + swap_planes(mid)
                g_row = mid + spread(rate[0][h], rate[1][h], k) * (sides - 6.0 * mid)
                cols = pl.ds(h * LANES, LANES)
                part[x0 + k, :, cols] = g_row
                to_l[g, k, :, cols] = jnp.concatenate([mid[:8], g_row[:8]], axis=0).astype(BF16)
                to_r[g, k, :, cols] = jnp.concatenate([mid[8:], g_row[8:]], axis=0).astype(BF16)
        to_l[g, 16] = d_ref[0, pl.ds(x0, 16), :].astype(BF16)
        to_r[g, 16] = d_ref[1, pl.ds(x0, 16), :].astype(BF16)
        return 0

    def span(c):
        a = 0 if c == 0 else c * (E // 16) + 1
        b = GROUPS if c == CHUNKS - 1 else (c + 1) * (E // 16) + 1
        return a, b - a

    def relay_copy(c, source, side):
        a, n = span(c)
        return pltpu.make_async_remote_copy(
            src_ref=source.at[pl.ds(a, n)],
            dst_ref=relayed.at[pl.ds(a, n)],
            send_sem=halo_send.at[side, c],
            recv_sem=relay_recv.at[c],
            device_id=(across, m),
            device_id_type=MESH,
        )

    def forward_copy(c, target, side):
        a, n = span(c)
        return pltpu.make_async_remote_copy(
            src_ref=relayed.at[pl.ds(a, n)],
            dst_ref=target.at[pl.ds(a, n)],
            send_sem=halo_send.at[side, c],
            recv_sem=halo_recv.at[side, c],
            device_id=(around, m),
            device_id_type=MESH,
        )

    def forward(c):
        if span(c)[1] == 0:
            return

        @pl.when(by_relay & (s == 0))
        def _():
            copy = forward_copy(c, from_r, 0)
            relay_copy(c, to_l, 0).wait_recv()
            copy.start()

        @pl.when(by_relay & (s == SPACE - 1))
        def _():
            copy = forward_copy(c, from_l, 1)
            relay_copy(c, to_r, 1).wait_recv()
            copy.start()

    def prepare():
        count = basis_ref.shape[0]
        basis = jnp.concatenate(
            [basis_ref[...].astype(F32), jnp.zeros((QP - count, LANES), F32)], axis=0
        ).astype(BF16)
        fill = jnp.zeros((1, QP - count), F32)

        def twice(row):
            return jnp.concatenate([row, fill, row, fill], axis=1)

        modes = lax.broadcasted_iota(jnp.int32, (DEV * 8, DEV * 16), 0)
        place = lax.broadcasted_iota(jnp.int32, (DEV * 8, DEV * 16), 1)
        base = place // 16 * 8 + place % 8
        level = (weight_ref[...] * base_ref[...])[None]
        swing = twice(level * slope_ref[...][None])
        level = twice(level)
        zero = jnp.zeros_like(basis)
        spread_out = 0.0
        for z in range(2):
            pick = jnp.where((modes == base) & (place % 16 // 8 == z), 1.0, 0.0).astype(BF16)
            w1[z * QP : (z + 1) * QP] = jnp.dot(basis, pick, preferred_element_type=F32).astype(BF16)
            rows = jnp.concatenate([basis, zero] if z == 0 else [zero, basis], axis=0)
            spread_out = spread_out + lax.dot_general(
                pick, rows, (((0,), (1,)), ((), ())), preferred_element_type=F32
            )
        w2[...] = (spread_out * swing).astype(BF16)
        total = jnp.sum(spread_out * level, axis=1, keepdims=True)
        bias[...] = jnp.broadcast_to(total, (DEV * 16, LANES))

    def halo_copies(c):
        a, n = span(c)
        if n == 0:
            return None, None
        left = pltpu.make_async_remote_copy(
            src_ref=to_l.at[pl.ds(a, n)],
            dst_ref=from_r.at[pl.ds(a, n)],
            send_sem=halo_send.at[0, c],
            recv_sem=halo_recv.at[0, c],
            device_id=(s - 1, m),
            device_id_type=MESH,
        )
        right = pltpu.make_async_remote_copy(
            src_ref=to_r.at[pl.ds(a, n)],
            dst_ref=from_l.at[pl.ds(a, n)],
            send_sem=halo_send.at[1, c],
            recv_sem=halo_recv.at[1, c],
            device_id=(s + 1, m),
            device_id_type=MESH,
        )
        return left, right

    @pl.when(s == 0)
    def _():
        def clear(g, _):
            from_l[g] = jnp.zeros((17, 16, NY), BF16)
            return 0

        lax.fori_loop(0, GROUPS, clear, 0)

    @pl.when(s == SPACE - 1)
    def _():
        def clear(g, _):
            from_r[g] = jnp.zeros((17, 16, NY), BF16)
            return 0

        lax.fori_loop(0, GROUPS, clear, 0)

    first[0] = jnp.zeros((16, NY), F32)
    first[NX + 1] = jnp.zeros((16, NY), F32)

    for c in range(CHUNKS):
        a, n = span(c)
        lax.fori_loop(a, a + n, sweep_group, 0)
        if c == 0:
            ends = jnp.where(is_end, 1, 0)
            pl.semaphore_wait(barrier, DEV + 1 - ends + jnp.where(by_relay, 2, 0))

        left, right = halo_copies(c)
        if left is None:
            continue
        relay = by_relay & is_far
        pl.when((s > 0) & jnp.logical_not(relay & (s == FAR)))(left.start)
        pl.when((s < SPACE - 1) & jnp.logical_not(relay & (s == FAR - 1)))(right.start)
        pl.when(relay & (s == FAR))(relay_copy(c, to_l, 0).start)
        pl.when(relay & (s == FAR - 1))(relay_copy(c, to_r, 1).start)

    forward(0)
    prepare()

    def finish_group(g, _):
        x0 = g * 16
        rate = [halves(d_ref[z, pl.ds(x0, 16), :]) for z in range(2)]
        for k in range(16):
            near_l, near_r = from_l[g, k], from_r[g, k]
            for h in range(2):
                cols = pl.ds(h * LANES, LANES)
                vl = near_l[:, h * LANES : (h + 1) * LANES].astype(F32)
                vr = near_r[:, h * LANES : (h + 1) * LANES].astype(F32)
                outer = jnp.concatenate([vl[:8], vr[:8]], axis=0)
                first[x0 + k + 1, :, cols] = (
                    part[x0 + k, :, cols] + spread(rate[0][h], rate[1][h], k) * outer
                )
        return 0

    def second_group(g, _):
        x0 = g * 16
        rate = [halves(d_ref[z, pl.ds(x0, 16), :]) for z in range(2)]
        outer_rate = [halves(ref[g, 16].astype(F32)) for ref in (from_l, from_r)]
        rows = [halves(first[x0 + k]) for k in range(18)]
        for k in range(16):
            here = rows[k + 1]
            across = beside_y(*here, first_lane, last_lane)
            v_row = row_of(v_ref, x0 + k)
            near_l, near_r = row_of(from_l.at[g], k), row_of(from_r.at[g], k)
            for h in range(2):
                mid = here[h]
                outer = jnp.concatenate([near_l[h][8:], near_r[h][8:]], axis=0)
                outer = outer + spread(outer_rate[0][h], outer_rate[1][h], k) * v_row[h]
                sides = rows[k][h] + rows[k + 2][h] + across[h] + swap_planes(mid) + outer
                value = mid + spread(rate[0][h], rate[1][h], k) * (sides - 6.0 * mid)
                settled[x0 + k, :, pl.ds(h * LANES, LANES)] = value.astype(BF16)
        return 0

    def fwd_copy(c, j, send=fwd_send, recv=fwd_recv):
        return pltpu.make_async_remote_copy(
            src_ref=settled.at[pl.ds(c * E + j * R, R)],
            dst_ref=gathered.at[c, m],
            send_sem=send.at[c],
            recv_sem=recv.at[c],
            device_id=(s, j),
            device_id_type=MESH,
        )

    def back_copy(c, j):
        return pltpu.make_async_remote_copy(
            src_ref=projected.at[c, j],
            dst_ref=returned.at[pl.ds(c * E + m * R, R)],
            send_sem=back_send.at[c],
            recv_sem=back_recv.at[c],
            device_id=(s, j),
            device_id_type=MESH,
        )

    def stage_stencil(c):
        for chunk in range(CHUNKS):

            @pl.when(c == chunk)
            def _():
                if chunk < CHUNKS - 1:
                    forward(chunk + 1)
                left, right = halo_copies(chunk)
                if left is not None:
                    pl.when(s < SPACE - 1)(left.wait_recv)
                    pl.when(s > 0)(right.wait_recv)
                    a, n = span(chunk)
                    lax.fori_loop(a, a + n, finish_group, 0)

        n = E // 16
        lax.fori_loop(c * n, (c + 1) * n, second_group, 0)

        def send(k, _):
            fwd_copy(c, lax.rem(m + k, DEV)).start()
            return 0

        lax.fori_loop(1, DEV, send, 0)
        pltpu.make_async_copy(
            settled.at[pl.ds(c * E + m * R, R)], gathered.at[c, m], fwd_recv.at[c]
        ).start()

    def stage_evaluate(c):
        pltpu.make_async_copy(gathered.at[c], gathered.at[c], fwd_recv.at[c]).wait()

        def one(r, _):
            cells = gathered[c, :, r].reshape(16 * DEV, NY)
            temp = jnp.dot(w1[...], cells, preferred_element_type=F32)
            heat = jnp.tanh(temp).astype(BF16)
            source = jnp.dot(w2[...], heat, preferred_element_type=F32)
            source = source + bias[:, :1]
            projected[c, :, r] = source.astype(BF16).reshape(DEV, 16, NY)
            return 0

        lax.fori_loop(0, R, one, 0)

        def send(k, _):
            back_copy(c, lax.rem(m + k, DEV)).start()
            return 0

        lax.fori_loop(1, DEV, send, 0)
        pltpu.make_async_copy(
            projected.at[c, m], returned.at[pl.ds(c * E + m * R, R)], back_recv.at[c]
        ).start()

    def stage_finish(c):
        rows = returned.at[pl.ds(c * E, E)]
        pltpu.make_async_copy(rows, rows, back_recv.at[c]).wait()

        def group(g, _):
            x0 = g * 16
            load = [halves(joule_ref[z, pl.ds(x0, 16), :]) for z in range(2)]
            rows = []
            for k in range(16):
                kept, source = row_of(settled, x0 + k), row_of(returned, x0 + k)
                value = [
                    kept[h] + spread(load[0][h], load[1][h], k) * source[h] for h in range(2)
                ]
                rows.append(jnp.concatenate(value, axis=1).astype(BF16))
            rows = jnp.concatenate(rows, axis=0)
            block = jnp.dot(swap[...], rows, preferred_element_type=F32).astype(BF16)
            out_ref[:, :, pl.ds(x0, 16), :] = block.reshape(2, 8, 16, NY)
            return 0

        n = E // 16
        lax.fori_loop(c * n, (c + 1) * n, group, 0)

    def step(t, _):
        @pl.when(t < CHUNKS)
        def _():
            stage_stencil(t)

        @pl.when((t >= 1) & (t < CHUNKS + 1))
        def _():
            stage_evaluate(t - 1)

        @pl.when(t >= 2)
        def _():
            stage_finish(t - 2)

        return 0

    lax.fori_loop(0, CHUNKS + 2, step, 0)

    for c in range(CHUNKS):
        left, right = halo_copies(c)
        if left is not None:
            pl.when((s > 0) | by_relay)(left.wait_send)
            pl.when((s < SPACE - 1) | by_relay)(right.wait_send)
        sent = settled.at[pl.ds(0, (DEV - 1) * R)]
        pltpu.make_async_copy(sent, sent, fwd_send.at[c]).wait()
        pltpu.make_async_copy(sent, sent, back_send.at[c]).wait()


def on_device(
    mode_field, diffusion, joule_load, chaos_basis, quad_weight, base_conductivity, thermal_slope
):
    vmem = pl.BlockSpec(memory_space=pltpu.VMEM)
    rows16 = (NX, 16, NY)
    halo = (GROUPS, 17, 16, NY)
    return pl.pallas_call(
        kernel,
        out_shape=jax.ShapeDtypeStruct(mode_field.shape, BF16),
        in_specs=[vmem] * 7,
        out_specs=vmem,
        scratch_shapes=[
            pltpu.VMEM(rows16, BF16),
            pltpu.VMEM((256, 256), BF16),
            pltpu.VMEM(halo, BF16),
            pltpu.VMEM(halo, BF16),
            pltpu.VMEM(halo, BF16),
            pltpu.VMEM(halo, BF16),
            pltpu.VMEM(halo, BF16),
            pltpu.VMEM(rows16, F32),
            pltpu.VMEM((NX + 2, 16, NY), F32),
            pltpu.VMEM(rows16, BF16),
            pltpu.VMEM((CHUNKS, DEV, R, 16, NY), BF16),
            pltpu.VMEM((CHUNKS, DEV, R, 16, NY), BF16),
            pltpu.VMEM(rows16, BF16),
            pltpu.VMEM((2 * QP, 2 * LANES), BF16),
            pltpu.VMEM((2 * LANES, 2 * QP), BF16),
            pltpu.VMEM((2 * LANES, LANES), F32),
            pltpu.SemaphoreType.DMA((2, CHUNKS)),
            pltpu.SemaphoreType.DMA((2, CHUNKS)),
            pltpu.SemaphoreType.DMA((CHUNKS,)),
            pltpu.SemaphoreType.DMA((CHUNKS,)),
            pltpu.SemaphoreType.DMA((CHUNKS,)),
            pltpu.SemaphoreType.DMA((CHUNKS,)),
            pltpu.SemaphoreType.DMA((CHUNKS,)),
        ],
        compiler_params=pltpu.CompilerParams(
            collective_id=0, has_side_effects=True, vmem_limit_bytes=56 * 2**20
        ),
        cost_estimate=pl.CostEstimate(
            flops=3 * 10**9, bytes_accessed=6 * 2**20, transcendentals=3 * 10**6
        ),
    )(
        mode_field,
        diffusion,
        joule_load,
        chaos_basis,
        quad_weight,
        base_conductivity,
        thermal_slope,
    )


def solution(mesh):
    return jax.shard_map(
        on_device,
        mesh=mesh,
        in_specs=(
            P("space", "modes", None, None),
            P("space", None, None),
            P("space", None, None),
            P(),
            P(),
            P(),
            P(),
        ),
        out_specs=P("space", "modes", None, None),
        check_vma=False,
    )
```

```python
import functools

import jax
import jax.numpy as jnp
from jax import lax
from jax.experimental import pallas as pl
from jax.experimental.pallas import tpu as pltpu
from jax.sharding import PartitionSpec as P

MESH = pl.DeviceIdType.MESH
F32 = jnp.float32
BF16 = jnp.bfloat16

NX = 256
NY = 256
LANES = 128
GROUPS = NX // 16
DEV = 16
SPACE = 32
FAR = SPACE // 2
CHUNKS = 8
E = NX // CHUNKS
R = E // DEV
PIECES = ((0, 64), (64, 64), (128, 128))
QP = 352


def halves(row):
    return row[..., :LANES], row[..., LANES:]


def beside_y(low, high, first_lane, last_lane):
    up_l, up_h = pltpu.roll(low, 1, 1), pltpu.roll(high, 1, 1)
    dn_l, dn_h = pltpu.roll(low, LANES - 1, 1), pltpu.roll(high, LANES - 1, 1)
    sum_l = jnp.where(first_lane, 0.0, up_l) + jnp.where(last_lane, dn_h, dn_l)
    sum_h = jnp.where(first_lane, up_l, up_h) + jnp.where(last_lane, 0.0, dn_h)
    return sum_l, sum_h


def swap_planes(a):
    return jnp.concatenate([a[8:], a[:8]], axis=0)


def spread(tile0, tile1, k):
    return jnp.concatenate(
        [
            jnp.broadcast_to(tile0[k : k + 1], (8, LANES)),
            jnp.broadcast_to(tile1[k : k + 1], (8, LANES)),
        ],
        axis=0,
    )


def kernel(
    field_hbm, d_ref, joule_ref, basis_ref, weight_ref, base_ref, slope_ref, out_ref,
    field_ref, v_ref, swap, load_sem,
    to_l, to_r, from_l, from_r, relayed, part, first, settled, gathered, projected, returned,
    w1, w2, bias,
    halo_send, halo_recv, relay_recv, fwd_send, fwd_recv, back_send, back_recv,
):
    s = lax.axis_index("space")
    m = lax.axis_index("modes")

    def load(i):
        rows = pl.ds(*PIECES[i])
        return pltpu.make_async_copy(
            field_hbm.at[:, :, rows, :], field_ref.at[:, :, rows, :], load_sem.at[i]
        )

    for i in range(len(PIECES)):
        load(i).start()

    barrier = pltpu.get_barrier_semaphore()

    def greet(k, _):
        pl.semaphore_signal(
            barrier, inc=1, device_id=(s, lax.rem(m + k, DEV)), device_id_type=MESH
        )
        return 0

    lax.fori_loop(1, DEV, greet, 0)

    @pl.when(s > 0)
    def _():
        pl.semaphore_signal(barrier, inc=1, device_id=(s - 1, m), device_id_type=MESH)

    @pl.when(s < SPACE - 1)
    def _():
        pl.semaphore_signal(barrier, inc=1, device_id=(s + 1, m), device_id_type=MESH)

    is_end = (s == 0) | (s == SPACE - 1)
    is_far = (s == FAR - 1) | (s == FAR)
    by_relay = (lax.rem(m, 2) == 1) & (is_end | is_far)
    across = lax.rem(s + FAR, SPACE)
    around = lax.rem(s // FAR * 2 * FAR + FAR + SPACE - 1 - s, SPACE)

    @pl.when(by_relay)
    def _():
        pl.semaphore_signal(barrier, inc=1, device_id=(across, m), device_id_type=MESH)
        pl.semaphore_signal(barrier, inc=1, device_id=(around, m), device_id_type=MESH)

    lane = lax.broadcasted_iota(jnp.int32, (16, LANES), 1)
    first_lane, last_lane = lane == 0, lane == LANES - 1

    def row_of(ref, x):
        return halves(ref[x].astype(F32))

    to_row = lax.broadcasted_iota(jnp.int32, (256, 256), 0)
    from_row = lax.broadcasted_iota(jnp.int32, (256, 256), 1)
    swapped = (to_row // 16 == from_row % 16) & (to_row % 16 == from_row // 16)
    swap[...] = jnp.where(swapped, 1.0, 0.0).astype(BF16)

    def regroup(g):
        x0 = g * 16
        block = field_ref[:, :, pl.ds(x0, 16), :].reshape(256, NY)
        rows = jnp.dot(swap[...], block, preferred_element_type=F32)
        v_ref[pl.ds(x0, 16)] = rows.astype(BF16).reshape(16, 16, NY)

    load(0).wait()
    regroup(0)

    def sweep_group(g, _):
        x0 = g * 16
        regroup(lax.rem(g + 1, GROUPS))
        before = row_of(v_ref, lax.rem(x0 + NX - 1, NX))
        before = tuple(jnp.where(g == 0, 0.0, b) for b in before)
        after = row_of(v_ref, lax.rem(x0 + 16, NX))
        after = tuple(jnp.where(g == GROUPS - 1, 0.0, a) for a in after)
        rows = [before] + [row_of(v_ref, x0 + k) for k in range(16)] + [after]
        rate = [halves(d_ref[z, pl.ds(x0, 16), :]) for z in range(2)]
        for k in range(16):
            here = rows[k + 1]
            across = beside_y(*here, first_lane, last_lane)
            for h in range(2):
                mid = here[h]
                sides = rows[k][h] + rows[k + 2][h] + across[h] + swap_planes(mid)
                g_row = mid + spread(rate[0][h], rate[1][h], k) * (sides - 6.0 * mid)
                cols = pl.ds(h * LANES, LANES)
                part[x0 + k, :, cols] = g_row
                to_l[g, k, :, cols] = jnp.concatenate([mid[:8], g_row[:8]], axis=0).astype(BF16)
                to_r[g, k, :, cols] = jnp.concatenate([mid[8:], g_row[8:]], axis=0).astype(BF16)
        to_l[g, 16] = d_ref[0, pl.ds(x0, 16), :].astype(BF16)
        to_r[g, 16] = d_ref[1, pl.ds(x0, 16), :].astype(BF16)
        return 0

    def span(c):
        a = 0 if c == 0 else c * (E // 16) + 1
        b = GROUPS if c == CHUNKS - 1 else (c + 1) * (E // 16) + 1
        return a, b - a

    def relay_copy(c, source, side):
        a, n = span(c)
        return pltpu.make_async_remote_copy(
            src_ref=source.at[pl.ds(a, n)],
            dst_ref=relayed.at[pl.ds(a, n)],
            send_sem=halo_send.at[side, c],
            recv_sem=relay_recv.at[c],
            device_id=(across, m),
            device_id_type=MESH,
        )

    def forward_copy(c, target, side):
        a, n = span(c)
        return pltpu.make_async_remote_copy(
            src_ref=relayed.at[pl.ds(a, n)],
            dst_ref=target.at[pl.ds(a, n)],
            send_sem=halo_send.at[side, c],
            recv_sem=halo_recv.at[side, c],
            device_id=(around, m),
            device_id_type=MESH,
        )

    def forward(c):
        if span(c)[1] == 0:
            return

        @pl.when(by_relay & (s == 0))
        def _():
            copy = forward_copy(c, from_r, 0)
            relay_copy(c, to_l, 0).wait_recv()
            copy.start()

        @pl.when(by_relay & (s == SPACE - 1))
        def _():
            copy = forward_copy(c, from_l, 1)
            relay_copy(c, to_r, 1).wait_recv()
            copy.start()

    def prepare():
        count = basis_ref.shape[0]
        basis = jnp.concatenate(
            [basis_ref[...].astype(F32), jnp.zeros((QP - count, LANES), F32)], axis=0
        ).astype(BF16)
        fill = jnp.zeros((1, QP - count), F32)

        def twice(row):
            return jnp.concatenate([row, fill, row, fill], axis=1)

        modes = lax.broadcasted_iota(jnp.int32, (DEV * 8, DEV * 16), 0)
        place = lax.broadcasted_iota(jnp.int32, (DEV * 8, DEV * 16), 1)
        base = place // 16 * 8 + place % 8
        level = (weight_ref[...] * base_ref[...])[None]
        swing = twice(level * slope_ref[...][None])
        level = twice(level)
        zero = jnp.zeros_like(basis)
        spread_out = 0.0
        for z in range(2):
            pick = jnp.where((modes == base) & (place % 16 // 8 == z), 1.0, 0.0).astype(BF16)
            w1[z * QP : (z + 1) * QP] = jnp.dot(basis, pick, preferred_element_type=F32).astype(BF16)
            rows = jnp.concatenate([basis, zero] if z == 0 else [zero, basis], axis=0)
            spread_out = spread_out + lax.dot_general(
                pick, rows, (((0,), (1,)), ((), ())), preferred_element_type=F32
            )
        w2[...] = (spread_out * swing).astype(BF16)
        total = jnp.sum(spread_out * level, axis=1, keepdims=True)
        bias[...] = jnp.broadcast_to(total, (DEV * 16, LANES))

    def halo_copies(c):
        a, n = span(c)
        if n == 0:
            return None, None
        left = pltpu.make_async_remote_copy(
            src_ref=to_l.at[pl.ds(a, n)],
            dst_ref=from_r.at[pl.ds(a, n)],
            send_sem=halo_send.at[0, c],
            recv_sem=halo_recv.at[0, c],
            device_id=(s - 1, m),
            device_id_type=MESH,
        )
        right = pltpu.make_async_remote_copy(
            src_ref=to_r.at[pl.ds(a, n)],
            dst_ref=from_l.at[pl.ds(a, n)],
            send_sem=halo_send.at[1, c],
            recv_sem=halo_recv.at[1, c],
            device_id=(s + 1, m),
            device_id_type=MESH,
        )
        return left, right

    @pl.when(s == 0)
    def _():
        def clear(g, _):
            from_l[g] = jnp.zeros((17, 16, NY), BF16)
            return 0

        lax.fori_loop(0, GROUPS, clear, 0)

    @pl.when(s == SPACE - 1)
    def _():
        def clear(g, _):
            from_r[g] = jnp.zeros((17, 16, NY), BF16)
            return 0

        lax.fori_loop(0, GROUPS, clear, 0)

    first[0] = jnp.zeros((16, NY), F32)
    first[NX + 1] = jnp.zeros((16, NY), F32)

    for c in range(CHUNKS):
        a, n = span(c)
        for i, (start, _) in enumerate(PIECES):
            if a * 16 < start <= (a + n) * 16 or (c == CHUNKS - 1 and start > (a + n) * 16):
                load(i).wait()
        lax.fori_loop(a, a + n, sweep_group, 0)
        if c == 0:
            ends = jnp.where(is_end, 1, 0)
            pl.semaphore_wait(barrier, DEV + 1 - ends + jnp.where(by_relay, 2, 0))

        left, right = halo_copies(c)
        if left is None:
            continue
        relay = by_relay & is_far
        pl.when((s > 0) & jnp.logical_not(relay & (s == FAR)))(left.start)
        pl.when((s < SPACE - 1) & jnp.logical_not(relay & (s == FAR - 1)))(right.start)
        pl.when(relay & (s == FAR))(relay_copy(c, to_l, 0).start)
        pl.when(relay & (s == FAR - 1))(relay_copy(c, to_r, 1).start)

    forward(0)
    prepare()

    def finish_group(g, _):
        x0 = g * 16
        rate = [halves(d_ref[z, pl.ds(x0, 16), :]) for z in range(2)]
        for k in range(16):
            near_l, near_r = from_l[g, k], from_r[g, k]
            for h in range(2):
                cols = pl.ds(h * LANES, LANES)
                vl = near_l[:, h * LANES : (h + 1) * LANES].astype(F32)
                vr = near_r[:, h * LANES : (h + 1) * LANES].astype(F32)
                outer = jnp.concatenate([vl[:8], vr[:8]], axis=0)
                first[x0 + k + 1, :, cols] = (
                    part[x0 + k, :, cols] + spread(rate[0][h], rate[1][h], k) * outer
                )
        return 0

    def second_group(g, _):
        x0 = g * 16
        rate = [halves(d_ref[z, pl.ds(x0, 16), :]) for z in range(2)]
        outer_rate = [halves(ref[g, 16].astype(F32)) for ref in (from_l, from_r)]
        rows = [halves(first[x0 + k]) for k in range(18)]
        for k in range(16):
            here = rows[k + 1]
            across = beside_y(*here, first_lane, last_lane)
            v_row = row_of(v_ref, x0 + k)
            near_l, near_r = row_of(from_l.at[g], k), row_of(from_r.at[g], k)
            for h in range(2):
                mid = here[h]
                outer = jnp.concatenate([near_l[h][8:], near_r[h][8:]], axis=0)
                outer = outer + spread(outer_rate[0][h], outer_rate[1][h], k) * v_row[h]
                sides = rows[k][h] + rows[k + 2][h] + across[h] + swap_planes(mid) + outer
                value = mid + spread(rate[0][h], rate[1][h], k) * (sides - 6.0 * mid)
                settled[x0 + k, :, pl.ds(h * LANES, LANES)] = value.astype(BF16)
        return 0

    def fwd_copy(c, j, send=fwd_send, recv=fwd_recv):
        return pltpu.make_async_remote_copy(
            src_ref=settled.at[pl.ds(c * E + j * R, R)],
            dst_ref=gathered.at[c, m],
            send_sem=send.at[c],
            recv_sem=recv.at[c],
            device_id=(s, j),
            device_id_type=MESH,
        )

    def back_copy(c, j):
        return pltpu.make_async_remote_copy(
            src_ref=projected.at[c, j],
            dst_ref=returned.at[pl.ds(c * E + m * R, R)],
            send_sem=back_send.at[c],
            recv_sem=back_recv.at[c],
            device_id=(s, j),
            device_id_type=MESH,
        )

    def stage_stencil(c):
        for chunk in range(CHUNKS):

            @pl.when(c == chunk)
            def _():
                if chunk < CHUNKS - 1:
                    forward(chunk + 1)
                left, right = halo_copies(chunk)
                if left is not None:
                    pl.when(s < SPACE - 1)(left.wait_recv)
                    pl.when(s > 0)(right.wait_recv)
                    a, n = span(chunk)
                    lax.fori_loop(a, a + n, finish_group, 0)

        n = E // 16
        lax.fori_loop(c * n, (c + 1) * n, second_group, 0)

        def send(k, _):
            fwd_copy(c, lax.rem(m + k, DEV)).start()
            return 0

        lax.fori_loop(1, DEV, send, 0)
        pltpu.make_async_copy(
            settled.at[pl.ds(c * E + m * R, R)], gathered.at[c, m], fwd_recv.at[c]
        ).start()

    def stage_evaluate(c):
        pltpu.make_async_copy(gathered.at[c], gathered.at[c], fwd_recv.at[c]).wait()

        def one(r, _):
            cells = gathered[c, :, r].reshape(16 * DEV, NY)
            temp = jnp.dot(w1[...], cells, preferred_element_type=F32)
            heat = jnp.tanh(temp).astype(BF16)
            source = jnp.dot(w2[...], heat, preferred_element_type=F32)
            source = source + bias[:, :1]
            projected[c, :, r] = source.astype(BF16).reshape(DEV, 16, NY)
            return 0

        lax.fori_loop(0, R, one, 0)

        def send(k, _):
            back_copy(c, lax.rem(m + k, DEV)).start()
            return 0

        lax.fori_loop(1, DEV, send, 0)
        pltpu.make_async_copy(
            projected.at[c, m], returned.at[pl.ds(c * E + m * R, R)], back_recv.at[c]
        ).start()

    def stage_finish(c):
        rows = returned.at[pl.ds(c * E, E)]
        pltpu.make_async_copy(rows, rows, back_recv.at[c]).wait()

        def group(g, _):
            x0 = g * 16
            load = [halves(joule_ref[z, pl.ds(x0, 16), :]) for z in range(2)]
            rows = []
            for k in range(16):
                kept, source = row_of(settled, x0 + k), row_of(returned, x0 + k)
                value = [
                    kept[h] + spread(load[0][h], load[1][h], k) * source[h] for h in range(2)
                ]
                rows.append(jnp.concatenate(value, axis=1).astype(BF16))
            rows = jnp.concatenate(rows, axis=0)
            block = jnp.dot(swap[...], rows, preferred_element_type=F32).astype(BF16)
            out_ref[:, :, pl.ds(x0, 16), :] = block.reshape(2, 8, 16, NY)
            return 0

        n = E // 16
        lax.fori_loop(c * n, (c + 1) * n, group, 0)

    def step(t, _):
        @pl.when(t < CHUNKS)
        def _():
            stage_stencil(t)

        @pl.when((t >= 1) & (t < CHUNKS + 1))
        def _():
            stage_evaluate(t - 1)

        @pl.when(t >= 2)
        def _():
            stage_finish(t - 2)

        return 0

    lax.fori_loop(0, CHUNKS + 2, step, 0)

    for c in range(CHUNKS):
        left, right = halo_copies(c)
        if left is not None:
            pl.when((s > 0) | by_relay)(left.wait_send)
            pl.when((s < SPACE - 1) | by_relay)(right.wait_send)
        sent = settled.at[pl.ds(0, (DEV - 1) * R)]
        pltpu.make_async_copy(sent, sent, fwd_send.at[c]).wait()
        pltpu.make_async_copy(sent, sent, back_send.at[c]).wait()


def on_device(
    mode_field, diffusion, joule_load, chaos_basis, quad_weight, base_conductivity, thermal_slope
):
    vmem = pl.BlockSpec(memory_space=pltpu.VMEM)
    rows16 = (NX, 16, NY)
    halo = (GROUPS, 17, 16, NY)
    anywhere = pl.BlockSpec(memory_space=pl.ANY)
    return pl.pallas_call(
        kernel,
        out_shape=pltpu.VMEM(mode_field.shape, BF16),
        in_specs=[anywhere] + [vmem] * 6,
        out_specs=vmem,
        scratch_shapes=[
            pltpu.VMEM(mode_field.shape, BF16),
            pltpu.VMEM(rows16, BF16),
            pltpu.VMEM((256, 256), BF16),
            pltpu.SemaphoreType.DMA((len(PIECES),)),
            pltpu.VMEM(halo, BF16),
            pltpu.VMEM(halo, BF16),
            pltpu.VMEM(halo, BF16),
            pltpu.VMEM(halo, BF16),
            pltpu.VMEM(halo, BF16),
            pltpu.VMEM(rows16, F32),
            pltpu.VMEM((NX + 2, 16, NY), F32),
            pltpu.VMEM(rows16, BF16),
            pltpu.VMEM((CHUNKS, DEV, R, 16, NY), BF16),
            pltpu.VMEM((CHUNKS, DEV, R, 16, NY), BF16),
            pltpu.VMEM(rows16, BF16),
            pltpu.VMEM((2 * QP, 2 * LANES), BF16),
            pltpu.VMEM((2 * LANES, 2 * QP), BF16),
            pltpu.VMEM((2 * LANES, LANES), F32),
            pltpu.SemaphoreType.DMA((2, CHUNKS)),
            pltpu.SemaphoreType.DMA((2, CHUNKS)),
            pltpu.SemaphoreType.DMA((CHUNKS,)),
            pltpu.SemaphoreType.DMA((CHUNKS,)),
            pltpu.SemaphoreType.DMA((CHUNKS,)),
            pltpu.SemaphoreType.DMA((CHUNKS,)),
            pltpu.SemaphoreType.DMA((CHUNKS,)),
        ],
        compiler_params=pltpu.CompilerParams(
            collective_id=0, has_side_effects=True, vmem_limit_bytes=56 * 2**20
        ),
        cost_estimate=pl.CostEstimate(
            flops=3 * 10**9, bytes_accessed=6 * 2**20, transcendentals=3 * 10**6
        ),
    )(
        mode_field,
        diffusion,
        joule_load,
        chaos_basis,
        quad_weight,
        base_conductivity,
        thermal_slope,
    )


def solution(mesh):
    return jax.shard_map(
        on_device,
        mesh=mesh,
        in_specs=(
            P("space", "modes", None, None),
            P("space", None, None),
            P("space", None, None),
            P(),
            P(),
            P(),
            P(),
        ),
        out_specs=P("space", "modes", None, None),
        check_vma=False,
    )
```
